768 devices in a mesh: row: 64 (over x, y, core), col: 12 (over z).
Axes of the slice: x: 4, y: 8, z: 12, core: 2. Of those that a mesh axis runs over, the one named last changes fastest.
Arguments:
- x_feat: bfloat16 [786432, 128], P(('row', 'col')), may hold values from -6 to 6
- weight: bfloat16 [128, 256], replicated, may hold values from -0.5 to 0.5
- tile_values: bfloat16 [61440, 128, 128], P(('row', 'col')), may hold values from 0 to 0.024169922
- tile_dst: int32 [61440], P(('row', 'col')), may hold values from 0 to 63
- tile_slot: int32 [61440], P(('row', 'col')), may hold values from 0 to 23, as said below
- src_blocks: int32 [9216, 2], P(('row', 'col')), may hold values from 0 to 7, as said below
- tile_count: int32 [768], P(('row', 'col')), may hold values from 10 to 80, as said below
- cotangent: bfloat16 [98304, 256], P(('row', 'col')), may hold values from -0.046875 to 0.046875
Outputs:
- layer_out: bfloat16 [98304, 256], P(('row', 'col'))
- weight_grad: float32 [128, 256], replicated
The draws below stay inside these ranges and needn't reach their ends.
Inputs may be any that keep to these rules, and one draw needn't show every extreme that they name: `tile_slot`: A tile names one of the 12 * 2 listed source blocks of its device. `src_blocks`: each row lists 2 distinct source blocks of one col peer. `tile_count`: some device has all 80 slots live.
All inputs are finite; a program needn't handle non-finite values.
Results may differ from the reference program's by a relative error of at most 0.0053.
Values may be sent and summed in bfloat16 or wider, within the bound.
No kernel may reach another device: no remote copies, remote signals or barrier semaphores. Data moves between devices by JAX's collectives and lax.ppermute only.
A program may use at most 32 MiB of HBM per device.

```python
import jax
import jax.numpy as jnp
from jax import lax

BLK = 128
D_IN = 128
HID = 256
DB_DEV = 1
SB_DEV = 8
NT = 80
CAP = 2
DST_COL = 64
NDST = 98304
NSRC = 786432
TILES = 61440
N_ROW = 64
N_COL = 12


def draw_tile_count(key, part):
    key = jax.random.fold_in(key, 11)
    first, second = jax.random.split(key)
    devices = N_ROW * N_COL
    levels = jnp.array([NT, NT // 2, NT // 4, NT // 8], jnp.int32)
    picks = jax.random.randint(first, (devices,), 0, 4)
    counts = levels[picks]
    fullest = jax.random.randint(second, (), 0, devices)
    counts = jnp.where(jnp.arange(devices) == fullest, NT, counts)
    return counts.astype(jnp.int32)


def draw_src_blocks(key, part):
    key = jax.random.fold_in(key, 23)
    total_rows = N_ROW * N_COL * N_COL
    scores = jax.random.randint(key, (total_rows, SB_DEV), 0, 1 << 20) * SB_DEV + jnp.arange(SB_DEV)[None, :]
    order = jnp.argsort(scores, axis=-1, stable=True)
    return order[:, :CAP].astype(jnp.int32)


def draw_tile_slot(key, part):
    key = jax.random.fold_in(key, 37)
    first, second = jax.random.split(key)
    devices = N_ROW * N_COL
    listed = N_COL * CAP
    places = jnp.arange(NT)
    filler = jax.random.randint(first, (devices, NT), 0, listed)
    slots = jnp.where(places[None, :] < listed, (places % listed)[None, :], filler)
    scores = jax.random.randint(second, (devices, NT), 0, 1 << 20) * NT + places[None, :]
    order = jnp.argsort(scores, axis=-1, stable=True)
    slots = jnp.take_along_axis(slots, order, axis=1)
    return slots.reshape(-1).astype(jnp.int32)


def with_ends(drawn, rng, low, high):
    index_at = [jax.random.randint(jax.random.fold_in(rng, axis), (), 0, length) for axis, length in enumerate(drawn.shape)]
    longest = drawn.shape.index(max(drawn.shape))
    next_to = index_at[:longest] + [(index_at[longest] + 1) % drawn.shape[longest]] + index_at[longest + 1:]
    return drawn.at[tuple(index_at)].set(low).at[tuple(next_to)].set(high)


def steps_of(rng, extent, cuts, least, top_value):
    loudness = 1.0
    for position, parts in cuts:
        draws = jax.random.uniform(jax.random.fold_in(jax.random.fold_in(rng, 6), position), (parts,), jnp.float32, least / len(cuts), top_value / len(cuts))
        loudness = loudness * jnp.repeat(jnp.exp(draws), extent[position] // parts).reshape((-1,) + (1,) * (len(extent) - 1 - position))
    return loudness


def centred(rng, extent, deviation, most, cuts=(), kind=jnp.bfloat16):
    result = jax.random.normal(rng, extent, jnp.float32) * deviation
    if len(cuts) > 0:
        result = steps_of(rng, extent, cuts, -0.22, 0.18) * result
    return jnp.clip(result, min=-most, max=most).astype(kind)


def setup_inputs(seed: int = 0) -> dict:
    streams_of = jax.random.split(jax.random.key(seed), 9)
    return {
        "x_feat": centred(streams_of[0], (NSRC, D_IN), 1.0, 6.0, ((0, 768),)),
        "weight": centred(streams_of[1], (D_IN, HID), D_IN ** -0.5, 0.5),
        "tile_values": jnp.clip(0.024169922 * jax.random.uniform(streams_of[2], (TILES, BLK, BLK), jnp.float32) ** steps_of(streams_of[2], (TILES, BLK, BLK), ((0, 768),), -0.2, 0.2), 0.0, 0.024169922).astype(jnp.bfloat16),
        "tile_dst": with_ends(jax.random.randint(streams_of[3], (TILES,), 0, DST_COL), jax.random.fold_in(streams_of[3], 1), 0, DST_COL - 1).astype(jnp.int32),
        "tile_slot": draw_tile_slot(jax.random.fold_in(streams_of[8], 71), 0),
        "src_blocks": draw_src_blocks(jax.random.fold_in(streams_of[8], 71), 0),
        "tile_count": draw_tile_count(jax.random.fold_in(streams_of[8], 71), 0),
        "cotangent": centred(streams_of[7], (NDST, HID), (NDST ** -0.5), 0.046875, ((0, 768),)),
    }


def reference(x_feat, weight, tile_values, tile_dst, tile_slot, src_blocks, tile_count, cotangent):
    devices = N_ROW * N_COL
    source_blocks = x_feat.reshape(devices * SB_DEV, BLK, D_IN)

    def visit(total, device):
        r = device // N_COL
        c = device % N_COL
        start = (device * NT).astype(jnp.int32)
        vals = lax.dynamic_slice_in_dim(tile_values, start, NT, 0).astype(jnp.float32)
        dst = lax.dynamic_slice_in_dim(tile_dst, start, NT, 0)
        slot = lax.dynamic_slice_in_dim(tile_slot, start, NT, 0)
        table = lax.dynamic_slice_in_dim(src_blocks, (device * N_COL).astype(jnp.int32), N_COL, 0)
        peer = slot // CAP
        local = table[peer, slot % CAP]
        source_index = ((r * N_COL + peer) * SB_DEV + local).astype(jnp.int32)
        target_index = (((dst // DB_DEV) * N_COL + c) * DB_DEV + dst % DB_DEV).astype(jnp.int32)
        live = (jnp.arange(NT, dtype=jnp.int32) < tile_count[device]).astype(jnp.float32)
        sources = source_blocks[source_index].astype(jnp.float32)
        product = jnp.einsum("tij,tjf->tif", vals, sources, precision=lax.Precision.HIGHEST)
        product = product * live[:, None, None]
        return total.at[target_index].add(product), None

    start_total = jnp.zeros((devices * DB_DEV, BLK, D_IN), jnp.float32)
    total, _ = lax.scan(visit, start_total, jnp.arange(devices, dtype=jnp.int32))
    aggregated = total.reshape(NDST, D_IN).astype(jnp.bfloat16)
    pre = jnp.dot(aggregated, weight, preferred_element_type=jnp.float32)
    sig = jax.nn.sigmoid(pre)
    layer_out = (pre * sig).astype(jnp.bfloat16)
    grad_pre = (cotangent.astype(jnp.float32) * sig * (1.0 + pre * (1.0 - sig))).astype(jnp.bfloat16)
    weight_grad = lax.dot_general(aggregated, grad_pre, (((0,), (0,)), ((), ())), preferred_element_type=jnp.float32)
    return layer_out, weight_grad
```

```python
import jax
import jax.numpy as jnp
from jax import lax
from jax.experimental import pallas as pl
from jax.experimental.pallas import tpu as pltpu
from jax.sharding import Mesh, PartitionSpec as P

BLK = 128
UNROLL = 8
AXES = ("x", "y", "core", "col")
ROW = ("x", "y", "core")
SIZES = (4, 8, 2, 12)

VMEM = pl.BlockSpec(memory_space=pltpu.VMEM)
SMEM = pl.BlockSpec(memory_space=pltpu.SMEM)
BF16 = jnp.bfloat16
F32 = jnp.float32


def pick_kernel(asked, x_ref, out_ref):
    peers, listed = out_ref.shape[0], out_ref.shape[1]
    for p in range(peers):
        for k in range(listed):
            out_ref[p, k] = x_ref[asked[p, 0, k]]


def pick(asked, x_feat):
    peers, listed = SIZES[3], 2
    return pl.pallas_call(
        pick_kernel,
        out_shape=jax.ShapeDtypeStruct((peers, listed, BLK, x_feat.shape[1]), BF16),
        in_specs=[SMEM, VMEM],
        out_specs=VMEM,
        name="pick_blocks",
    )(asked, x_feat.reshape(-1, BLK, x_feat.shape[1]))


def aggregate_kernel(dst, slot, count, core, tiles, sources, mine, theirs, acc):
    half = mine.shape[0]
    live = count[0]
    me = core[0]
    acc[...] = jnp.zeros_like(acc)

    def group(g, carry):
        for u in range(UNROLL):
            t = g * UNROLL + u
            d = dst[t]
            place = ((d & 1) ^ me) * half + (d >> 1)
            place = jnp.where(t < live, place, 2 * half)
            acc[place] += jnp.dot(tiles[t], sources[slot[t]], preferred_element_type=F32)
        return carry

    lax.fori_loop(0, (live + (UNROLL - 1)) >> 3, group, 0)
    mine[...] = acc[pl.ds(0, half)]
    theirs[...] = acc[pl.ds(half, half)].astype(BF16)


def aggregate(dst, slot, count, core, tiles, sources):
    half = 32
    d_in = sources.shape[-1]
    return pl.pallas_call(
        aggregate_kernel,
        out_shape=(
            jax.ShapeDtypeStruct((half, BLK, d_in), F32),
            jax.ShapeDtypeStruct((half, BLK, d_in), BF16),
        ),
        in_specs=[SMEM, SMEM, SMEM, SMEM, VMEM, VMEM],
        out_specs=(VMEM, VMEM),
        scratch_shapes=[pltpu.VMEM((2 * half + 1, BLK, d_in), F32)],
        compiler_params=pltpu.CompilerParams(vmem_limit_bytes=32 * 1024 * 1024),
        name="aggregate_tiles",
    )(dst, slot, count, core, tiles, sources)


def layer_kernel(terms, weight, cotangent, out, grad):
    total = terms[0].astype(F32)
    for i in range(1, terms.shape[0]):
        total = total + terms[i].astype(F32)
    aggregated = total.astype(BF16)
    pre = jnp.dot(aggregated, weight[...], preferred_element_type=F32)
    sig = jax.nn.sigmoid(pre)
    out[...] = (pre * sig).astype(BF16)
    grad_pre = (cotangent[...].astype(F32) * sig * (1.0 + pre * (1.0 - sig))).astype(BF16)
    for h in range(2):
        grad[h] = lax.dot_general(
            aggregated,
            grad_pre[:, h * 128 : (h + 1) * 128],
            (((0,), (0,)), ((), ())),
            preferred_element_type=F32,
        )


def layer(terms, weight, cotangent):
    return pl.pallas_call(
        layer_kernel,
        out_shape=(
            jax.ShapeDtypeStruct(cotangent.shape, BF16),
            jax.ShapeDtypeStruct((2, BLK, 128), F32),
        ),
        in_specs=[VMEM, VMEM, VMEM],
        out_specs=(VMEM, VMEM),
        name="layer",
    )(terms, weight, cotangent)


def exchange(a, axis):
    return lax.all_to_all(a, axis, 0, 0, tiled=True)


def body(x_feat, weight, tile_values, tile_dst, tile_slot, src_blocks, tile_count, cotangent):
    d_in = x_feat.shape[1]
    xs, ys, cores, cols = SIZES
    with jax.named_scope("ask"):
        listed = jnp.pad(src_blocks, ((0, 0), (0, 126))).reshape(cols, 1, 128)
        asked = exchange(listed, "col")
    with jax.named_scope("pick"):
        picked = pick(asked, x_feat)
    with jax.named_scope("sources"):
        sources = exchange(picked.reshape(cols, 2 * BLK, d_in), "col")
        sources = sources.reshape(cols * 2, BLK, d_in)
    with jax.named_scope("aggregate"):
        core = lax.axis_index("core").astype(jnp.int32).reshape(1)
        mine, theirs = aggregate(tile_dst, tile_slot, tile_count, core, tile_values, sources)
    with jax.named_scope("sum_core"):
        other = lax.ppermute(theirs, "core", [(0, 1), (1, 0)])
        summed = (mine + other.astype(F32)).astype(BF16)
    with jax.named_scope("sum_x"):
        got = exchange(summed.reshape(xs, ys * BLK, d_in), "x")
        summed = jnp.sum(got.astype(F32), axis=0).astype(BF16)
    with jax.named_scope("sum_y"):
        terms = exchange(summed.reshape(ys, BLK, d_in), "y")
    with jax.named_scope("layer"):
        layer_out, grad = layer(terms, weight, cotangent)
    with jax.named_scope("grad_row"):
        part = jnp.sum(exchange(grad.reshape(64, 4, 128), ROW), axis=0)
    with jax.named_scope("grad_col"):
        part = jnp.sum(exchange(jnp.broadcast_to(part[None], (cols, 4, 128)), "col"), axis=0)
    with jax.named_scope("grad_all"):
        whole = exchange(jnp.broadcast_to(part[None], (64, 4, 128)), ROW)
        whole = whole.reshape(2, BLK, 128)
        weight_grad = jnp.concatenate([whole[0], whole[1]], axis=1)
    return (layer_out, weight_grad)


def solution(mesh):
    grid = Mesh(mesh.devices.reshape(SIZES), AXES)
    return jax.shard_map(
        body,
        mesh=grid,
        in_specs=(
            P(AXES, None),
            P(),
            P(AXES, None, None),
            P(AXES),
            P(AXES),
            P(AXES, None),
            P(AXES),
            P(AXES, None),
        ),
        out_specs=(P(AXES, None), P()),
        check_vma=False,
    )
```

```python
import jax
import jax.numpy as jnp
from jax import lax
from jax.experimental import pallas as pl
from jax.experimental.pallas import tpu as pltpu
from jax.sharding import Mesh, PartitionSpec as P

BLK = 128
UNROLL = 8
AXES = ("x", "y", "core", "col")
SIZES = (4, 8, 2, 12)

VMEM = pl.BlockSpec(memory_space=pltpu.VMEM)
SMEM = pl.BlockSpec(memory_space=pltpu.SMEM)
BF16 = jnp.bfloat16
F32 = jnp.float32


def pick_kernel(asked, x_ref, out_ref):
    peers, listed = out_ref.shape[0], out_ref.shape[1]
    for p in range(peers):
        for k in range(listed):
            out_ref[p, k] = x_ref[(asked[p, 0, 0] >> (8 * k)) & 255]


def pick(asked, x_feat):
    peers, listed = SIZES[3], 2
    return pl.pallas_call(
        pick_kernel,
        out_shape=jax.ShapeDtypeStruct((peers, listed, BLK, x_feat.shape[1]), BF16),
        in_specs=[SMEM, VMEM],
        out_specs=VMEM,
        compiler_params=pltpu.CompilerParams(vmem_limit_bytes=4 * 1024 * 1024),
        name="pick_blocks",
    )(asked, x_feat.reshape(-1, BLK, x_feat.shape[1]))


def aggregate_kernel(dst, slot, count, core, tiles, sources, mine, theirs, acc):
    half = mine.shape[0]
    live = count[0]
    me = core[0]
    acc[...] = jnp.zeros_like(acc)

    def group(g, carry):
        for u in range(UNROLL):
            t = g * UNROLL + u
            d = dst[t]
            place = ((d & 1) ^ me) * half + (d >> 1)
            place = jnp.where(t < live, place, 2 * half)
            acc[place] += jnp.dot(tiles[t], sources[slot[t]], preferred_element_type=F32)
        return carry

    lax.fori_loop(0, (live + (UNROLL - 1)) >> 3, group, 0)
    mine[...] = acc[pl.ds(0, half)]
    theirs[...] = acc[pl.ds(half, half)].astype(BF16)


def aggregate(dst, slot, count, core, tiles, sources):
    half = 32
    d_in = sources.shape[-1]
    return pl.pallas_call(
        aggregate_kernel,
        out_shape=(
            jax.ShapeDtypeStruct((half, BLK, d_in), F32),
            jax.ShapeDtypeStruct((half, BLK, d_in), BF16),
        ),
        in_specs=[SMEM, SMEM, SMEM, SMEM, VMEM, VMEM],
        out_specs=(VMEM, VMEM),
        scratch_shapes=[pltpu.VMEM((2 * half + 1, BLK, d_in), F32)],
        compiler_params=pltpu.CompilerParams(vmem_limit_bytes=16 * 1024 * 1024),
        name="aggregate_tiles",
    )(dst, slot, count, core, tiles, sources)


def layer_kernel(terms, weight, cotangent, out, grad):
    aggregated = add_all(terms).astype(BF16)
    pre = jnp.dot(aggregated, weight[...], preferred_element_type=F32)
    sig = jax.nn.sigmoid(pre)
    out[...] = (pre * sig).astype(BF16)
    grad_pre = (cotangent[...].astype(F32) * sig * (1.0 + pre * (1.0 - sig))).astype(BF16)
    for h in range(2):
        grad[h] = lax.dot_general(
            aggregated,
            grad_pre[:, h * 128 : (h + 1) * 128],
            (((0,), (0,)), ((), ())),
            preferred_element_type=F32,
        )


def layer(terms, weight, cotangent):
    return pl.pallas_call(
        layer_kernel,
        out_shape=(
            jax.ShapeDtypeStruct(cotangent.shape, BF16),
            jax.ShapeDtypeStruct((2, BLK, 128), F32),
        ),
        in_specs=[VMEM, VMEM, VMEM],
        out_specs=(VMEM, VMEM),
        compiler_params=pltpu.CompilerParams(vmem_limit_bytes=4 * 1024 * 1024),
        name="layer",
    )(terms, weight, cotangent)


def exchange(a, axis):
    return lax.all_to_all(a, axis, 0, 0, tiled=True)


def add_all(terms):
    total = terms[0].astype(F32)
    for i in range(1, terms.shape[0]):
        total = total + terms[i].astype(F32)
    return total


def body(x_feat, weight, tile_values, tile_dst, tile_slot, src_blocks, tile_count, cotangent):
    d_in = x_feat.shape[1]
    xs, ys, cores, cols = SIZES
    with jax.named_scope("ask"):
        pair = src_blocks[:, 0] + 256 * src_blocks[:, 1]
        asked = exchange(jnp.broadcast_to(pair[:, None, None], (cols, 1, 128)), "col")
    with jax.named_scope("pick"):
        picked = pick(asked, x_feat)
    with jax.named_scope("sources"):
        sources = exchange(picked.reshape(cols, 2 * BLK, d_in), "col")
        sources = sources.reshape(cols * 2, BLK, d_in)
    with jax.named_scope("aggregate"):
        core = lax.axis_index("core").astype(jnp.int32).reshape(1)
        mine, theirs = aggregate(tile_dst, tile_slot, tile_count, core, tile_values, sources)
    with jax.named_scope("sum_core"):
        other = lax.ppermute(theirs, "core", [(0, 1), (1, 0)])
        summed = (mine + other.astype(F32)).astype(BF16)
    with jax.named_scope("sum_x"):
        got = exchange(summed.reshape(xs, ys * BLK, d_in), "x")
        summed = add_all(got).astype(BF16)
    with jax.named_scope("sum_y"):
        terms = exchange(summed.reshape(ys, BLK, d_in), "y")
    with jax.named_scope("layer"):
        layer_out, grad = layer(terms, weight, cotangent)
    with jax.named_scope("grad_xy"):
        part = jnp.sum(exchange(grad.reshape(32, 8, 128), ("x", "y")), axis=0)
    with jax.named_scope("grad_core_col"):
        part = jnp.broadcast_to(part[None], (24, 8, 128))
        part = jnp.sum(exchange(part, ("core", "col")), axis=0)
    with jax.named_scope("grad_all"):
        whole = exchange(jnp.broadcast_to(part[None], (32, 8, 128)), ("x", "y"))
        whole = whole.reshape(2, BLK, 128)
        weight_grad = jnp.concatenate([whole[0], whole[1]], axis=1)
    return (layer_out, weight_grad)


def solution(mesh):
    grid = Mesh(mesh.devices.reshape(SIZES), AXES)
    return jax.shard_map(
        body,
        mesh=grid,
        in_specs=(
            P(AXES, None),
            P(),
            P(AXES, None, None),
            P(AXES),
            P(AXES),
            P(AXES, None),
            P(AXES),
            P(AXES, None),
        ),
        out_specs=(P(AXES, None), P()),
        check_vma=False,
    )
```

```python
import jax
import jax.numpy as jnp
from jax import lax
from jax.experimental import pallas as pl
from jax.experimental.pallas import tpu as pltpu
from jax.sharding import Mesh, PartitionSpec as P

BLK = 128
UNROLL = 20
AXES = ("x", "far", "near", "core", "col")
SIZES = (4, 4, 2, 2, 12)

VMEM = pl.BlockSpec(memory_space=pltpu.VMEM)
SMEM = pl.BlockSpec(memory_space=pltpu.SMEM)
BF16 = jnp.bfloat16
F32 = jnp.float32


def pick_kernel(asked, x_ref, out_ref):
    peers, listed = out_ref.shape[0], out_ref.shape[1]
    for p in range(peers):
        for k in range(listed):
            out_ref[p, k] = x_ref[(asked[p, 0, 0] >> (8 * k)) & 255]


def pick(asked, x_feat):
    peers, listed = SIZES[4], 2
    return pl.pallas_call(
        pick_kernel,
        out_shape=jax.ShapeDtypeStruct((peers, listed, BLK, x_feat.shape[1]), BF16),
        in_specs=[SMEM, VMEM],
        out_specs=VMEM,
        name="pick_blocks",
    )(asked, x_feat.reshape(-1, BLK, x_feat.shape[1]))


def aggregate_kernel(dst, slot, count, core, tiles, sources, acc, theirs):
    half = theirs.shape[0]
    live = count[0]
    me = core[0]
    acc[...] = jnp.zeros_like(acc)

    def group(g, carry):
        for u in range(UNROLL):
            t = g * UNROLL + u
            d = dst[t]
            xy = (d & 0x30) | ((d & 2) << 2) | ((d & 0xC) >> 1)
            place = ((d & 1) ^ me) * half + (xy >> 1)
            place = jnp.where(t < live, place, 2 * half)
            acc[place] += jnp.dot(tiles[t], sources[slot[t]], preferred_element_type=F32)
        return carry

    lax.fori_loop(0, lax.div(live + (UNROLL - 1), UNROLL), group, 0)
    theirs[...] = acc[pl.ds(half, half)].astype(BF16)


def aggregate(dst, slot, count, core, tiles, sources):
    half = 32
    d_in = sources.shape[-1]
    return pl.pallas_call(
        aggregate_kernel,
        out_shape=(
            jax.ShapeDtypeStruct((2 * half + 1, BLK, d_in), F32),
            jax.ShapeDtypeStruct((half, BLK, d_in), BF16),
        ),
        in_specs=[SMEM, SMEM, SMEM, SMEM, VMEM, VMEM],
        out_specs=(VMEM, VMEM),
        compiler_params=pltpu.CompilerParams(vmem_limit_bytes=16 * 1024 * 1024),
        name="aggregate_tiles",
    )(dst, slot, count, core, tiles, sources)


def layer_kernel(terms, weight, cotangent, out, grad):
    aggregated = add_all(terms).astype(BF16)
    pre = jnp.dot(aggregated, weight[...], preferred_element_type=F32)
    sig = jax.nn.sigmoid(pre)
    out[...] = (pre * sig).astype(BF16)
    grad_pre = (cotangent[...].astype(F32) * sig * (1.0 + pre * (1.0 - sig))).astype(BF16)
    for h in range(2):
        grad[h] = lax.dot_general(
            aggregated,
            grad_pre[:, h * 128 : (h + 1) * 128],
            (((0,), (0,)), ((), ())),
            preferred_element_type=F32,
        )


def layer(terms, weight, cotangent):
    return pl.pallas_call(
        layer_kernel,
        out_shape=(
            jax.ShapeDtypeStruct(cotangent.shape, BF16),
            jax.ShapeDtypeStruct((2, BLK, 128), F32),
        ),
        in_specs=[VMEM, VMEM, VMEM],
        out_specs=(VMEM, VMEM),
        compiler_params=pltpu.CompilerParams(vmem_limit_bytes=4 * 1024 * 1024),
        name="layer",
    )(terms, weight, cotangent)


def exchange(a, axis):
    return lax.all_to_all(a, axis, 0, 0, tiled=True)


def add_all(terms):
    total = terms[0].astype(F32)
    for i in range(1, terms.shape[0]):
        total = total + terms[i].astype(F32)
    return total


def body(x_feat, weight, tile_values, tile_dst, tile_slot, src_blocks, tile_count, cotangent):
    d_in = x_feat.shape[1]
    xs, fars, nears, cores, cols = SIZES
    with jax.named_scope("ask"):
        pair = src_blocks[:, 0] + 256 * src_blocks[:, 1]
        asked = exchange(jnp.broadcast_to(pair[:, None, None], (cols, 1, 128)), "col")
    with jax.named_scope("pick"):
        picked = pick(asked, x_feat)
    with jax.named_scope("sources"):
        sources = exchange(picked.reshape(cols, 2 * BLK, d_in), "col")
        sources = sources.reshape(cols * 2, BLK, d_in)
    with jax.named_scope("aggregate"):
        core = lax.axis_index("core").astype(jnp.int32).reshape(1)
        mine, theirs = aggregate(tile_dst, tile_slot, tile_count, core, tile_values, sources)
    with jax.named_scope("sum_core"):
        other = lax.ppermute(theirs, "core", [(0, 1), (1, 0)])
        summed = (mine[: other.shape[0]] + other.astype(F32)).astype(BF16)
    with jax.named_scope("sum_x_near"):
        got = exchange(summed.reshape(xs * nears, fars * BLK, d_in), ("x", "near"))
        summed = add_all(got).astype(BF16)
    with jax.named_scope("sum_far"):
        terms = exchange(summed.reshape(fars, BLK, d_in), "far")
    with jax.named_scope("layer"):
        layer_out, grad = layer(terms, weight, cotangent)
    with jax.named_scope("grad_xy"):
        part = jnp.sum(exchange(grad.reshape(32, 8, 128), ("x", "far", "near")), axis=0)
    with jax.named_scope("grad_core_col"):
        part = jnp.broadcast_to(part[None], (24, 8, 128))
        part = jnp.sum(exchange(part, ("core", "col")), axis=0)
    with jax.named_scope("grad_all"):
        whole = exchange(jnp.broadcast_to(part[None], (32, 8, 128)), ("x", "far", "near"))
        whole = whole.reshape(2, BLK, 128)
        weight_grad = jnp.concatenate([whole[0], whole[1]], axis=1)
    return (layer_out, weight_grad)


def solution(mesh):
    grid = Mesh(mesh.devices.reshape(SIZES), AXES)
    return jax.shard_map(
        body,
        mesh=grid,
        in_specs=(
            P(AXES, None),
            P(),
            P(AXES, None, None),
            P(AXES),
            P(AXES),
            P(AXES, None),
            P(AXES),
            P(AXES, None),
        ),
        out_specs=(P(AXES, None), P()),
        check_vma=False,
    )
```

```python
import jax
import jax.numpy as jnp
from jax import lax
from jax.experimental import pallas as pl
from jax.experimental.pallas import tpu as pltpu
from jax.sharding import Mesh, PartitionSpec as P

BLK = 128
UNROLL = 20
AXES = ("x", "far", "near", "core", "col")
SIZES = (4, 4, 2, 2, 12)

VMEM = pl.BlockSpec(memory_space=pltpu.VMEM)
SMEM = pl.BlockSpec(memory_space=pltpu.SMEM)
BF16 = jnp.bfloat16
F32 = jnp.float32


def pick_kernel(asked, x_ref, out_ref):
    peers, listed = out_ref.shape[0], out_ref.shape[1]
    for p in range(peers):
        for k in range(listed):
            out_ref[p, k] = x_ref[(asked[p, 0, 0] >> (8 * k)) & 255]


def pick(asked, x_feat):
    peers, listed = SIZES[4], 2
    return pl.pallas_call(
        pick_kernel,
        out_shape=jax.ShapeDtypeStruct((peers, listed, BLK, x_feat.shape[1]), BF16),
        in_specs=[SMEM, VMEM],
        out_specs=VMEM,
        name="pick_blocks",
    )(asked, x_feat.reshape(-1, BLK, x_feat.shape[1]))


def aggregate_kernel(dst, slot, count, core, tiles, sources, acc, theirs):
    half = theirs.shape[0]
    live = count[0]
    me = core[0]
    acc[...] = jnp.zeros_like(acc)

    def group(g, carry):
        for u in range(UNROLL):
            t = g * UNROLL + u
            d = dst[t]
            xy = (d & 0x30) | ((d & 2) << 2) | ((d & 0xC) >> 1)
            place = ((d & 1) ^ me) * half + (xy >> 1)
            place = jnp.where(t < live, place, 2 * half)
            acc[place] += jnp.dot(tiles[t], sources[slot[t]], preferred_element_type=F32)
        return carry

    lax.fori_loop(0, lax.div(live + (UNROLL - 1), UNROLL), group, 0)
    theirs[...] = acc[pl.ds(half, half)].astype(BF16)


def aggregate(dst, slot, count, core, tiles, sources):
    half = 32
    d_in = sources.shape[-1]
    return pl.pallas_call(
        aggregate_kernel,
        out_shape=(
            jax.ShapeDtypeStruct((2 * half + 1, BLK, d_in), F32),
            jax.ShapeDtypeStruct((half, BLK, d_in), BF16),
        ),
        in_specs=[SMEM, SMEM, SMEM, SMEM, VMEM, VMEM],
        out_specs=(VMEM, VMEM),
        compiler_params=pltpu.CompilerParams(vmem_limit_bytes=16 * 1024 * 1024),
        name="aggregate_tiles",
    )(dst, slot, count, core, tiles, sources)


def layer_kernel(terms, weight, cotangent, out, grad):
    aggregated = add_all(terms).astype(BF16)
    pre = jnp.dot(aggregated, weight[...], preferred_element_type=F32)
    sig = jax.nn.sigmoid(pre)
    out[...] = (pre * sig).astype(BF16)
    grad_pre = (cotangent[...].astype(F32) * sig * (1.0 + pre * (1.0 - sig))).astype(BF16)
    for h in range(2):
        grad[h] = lax.dot_general(
            aggregated,
            grad_pre[:, h * 128 : (h + 1) * 128],
            (((0,), (0,)), ((), ())),
            preferred_element_type=F32,
        ).astype(BF16)


def layer(terms, weight, cotangent):
    return pl.pallas_call(
        layer_kernel,
        out_shape=(
            jax.ShapeDtypeStruct(cotangent.shape, BF16),
            jax.ShapeDtypeStruct((2, BLK, 128), BF16),
        ),
        in_specs=[VMEM, VMEM, VMEM],
        out_specs=(VMEM, VMEM),
        compiler_params=pltpu.CompilerParams(vmem_limit_bytes=4 * 1024 * 1024),
        name="layer",
    )(terms, weight, cotangent)


def exchange(a, axis):
    return lax.all_to_all(a, axis, 0, 0, tiled=True)


def add_all(terms):
    total = terms[0].astype(F32)
    for i in range(1, terms.shape[0]):
        total = total + terms[i].astype(F32)
    return total


def body(x_feat, weight, tile_values, tile_dst, tile_slot, src_blocks, tile_count, cotangent):
    d_in = x_feat.shape[1]
    xs, fars, nears, cores, cols = SIZES
    with jax.named_scope("ask"):
        pair = src_blocks[:, 0] + 256 * src_blocks[:, 1]
        asked = exchange(jnp.broadcast_to(pair[:, None, None], (cols, 1, 128)), "col")
    with jax.named_scope("pick"):
        picked = pick(asked, x_feat)
    with jax.named_scope("sources"):
        sources = exchange(picked.reshape(cols, 2 * BLK, d_in), "col")
        sources = sources.reshape(cols * 2, BLK, d_in)
    with jax.named_scope("aggregate"):
        core = lax.axis_index("core").astype(jnp.int32).reshape(1)
        mine, theirs = aggregate(tile_dst, tile_slot, tile_count, core, tile_values, sources)
    with jax.named_scope("sum_core"):
        other = lax.ppermute(theirs, "core", [(0, 1), (1, 0)])
        summed = (mine[: other.shape[0]] + other.astype(F32)).astype(BF16)
    with jax.named_scope("sum_x_near"):
        got = exchange(summed.reshape(xs * nears, fars * BLK, d_in), ("x", "near"))
        summed = add_all(got).astype(BF16)
    with jax.named_scope("sum_far"):
        terms = exchange(summed.reshape(fars, BLK, d_in), "far")
    with jax.named_scope("layer"):
        layer_out, grad = layer(terms, weight, cotangent)
    with jax.named_scope("grad_xy"):
        part = add_all(exchange(grad.reshape(32, 8, 128), ("x", "far", "near")))
    with jax.named_scope("grad_core_col"):
        part = jnp.broadcast_to(part[None], (24, 8, 128))
        part = jnp.sum(exchange(part, ("core", "col")), axis=0)
    with jax.named_scope("grad_all"):
        whole = exchange(jnp.broadcast_to(part[None], (32, 8, 128)), ("x", "far", "near"))
        whole = whole.reshape(2, BLK, 128)
        weight_grad = jnp.concatenate([whole[0], whole[1]], axis=1)
    return (layer_out, weight_grad)


def solution(mesh):
    grid = Mesh(mesh.devices.reshape(SIZES), AXES)
    return jax.shard_map(
        body,
        mesh=grid,
        in_specs=(
            P(AXES, None),
            P(),
            P(AXES, None, None),
            P(AXES),
            P(AXES),
            P(AXES, None),
            P(AXES),
            P(AXES, None),
        ),
        out_specs=(P(AXES, None), P()),
        check_vma=False,
    )
```

```python
import jax
import jax.numpy as jnp
from jax import lax
from jax.experimental import pallas as pl
from jax.experimental.pallas import tpu as pltpu
from jax.sharding import Mesh, PartitionSpec as P

BLK = 128
UNROLL = 20
AXES = ("x", "far", "near", "core", "col")
SIZES = (4, 4, 2, 2, 12)

VMEM = pl.BlockSpec(memory_space=pltpu.VMEM)
SMEM = pl.BlockSpec(memory_space=pltpu.SMEM)
BF16 = jnp.bfloat16
F32 = jnp.float32


def pick_kernel(asked, x_ref, out_ref):
    peers, listed = out_ref.shape[0], out_ref.shape[1]
    for p in range(peers):
        for k in range(listed):
            out_ref[p, k] = x_ref[(asked[p, 0, 0] >> (8 * k)) & 255]


def pick(asked, x_feat):
    peers, listed = SIZES[4], 2
    return pl.pallas_call(
        pick_kernel,
        out_shape=jax.ShapeDtypeStruct((peers, listed, BLK, x_feat.shape[1]), BF16),
        in_specs=[SMEM, VMEM],
        out_specs=VMEM,
        name="pick_blocks",
    )(asked, x_feat.reshape(-1, BLK, x_feat.shape[1]))


def aggregate_kernel(dst, slot, count, core, tiles, sources, acc, theirs):
    half = theirs.shape[0]
    live = count[0]
    me = core[0]
    acc[...] = jnp.zeros_like(acc)

    def group(g, carry):
        for u in range(UNROLL):
            t = g * UNROLL + u
            d = dst[t]
            xy = (d & 0x30) | ((d & 2) << 2) | ((d & 0xC) >> 1)
            place = ((d & 1) ^ me) * half + (xy >> 1)
            place = jnp.where(t < live, place, 2 * half)
            acc[place] += jnp.dot(tiles[t], sources[slot[t]], preferred_element_type=F32)
        return carry

    lax.fori_loop(0, lax.div(live + (UNROLL - 1), UNROLL), group, 0)
    theirs[...] = acc[pl.ds(half, half)].astype(BF16)


def aggregate(dst, slot, count, core, tiles, sources):
    half = 32
    d_in = sources.shape[-1]
    return pl.pallas_call(
        aggregate_kernel,
        out_shape=(
            jax.ShapeDtypeStruct((2 * half + 1, BLK, d_in), F32),
            jax.ShapeDtypeStruct((half, BLK, d_in), BF16),
        ),
        in_specs=[SMEM, SMEM, SMEM, SMEM, VMEM, VMEM],
        out_specs=(VMEM, VMEM),
        compiler_params=pltpu.CompilerParams(vmem_limit_bytes=16 * 1024 * 1024),
        name="aggregate_tiles",
    )(dst, slot, count, core, tiles, sources)


def layer_kernel(terms, weight, cotangent, out, grad):
    aggregated = add_all(terms).astype(BF16)
    pre = jnp.dot(aggregated, weight[...], preferred_element_type=F32)
    sig = jax.nn.sigmoid(pre)
    out[...] = (pre * sig).astype(BF16)
    grad_pre = (cotangent[...].astype(F32) * sig * (1.0 + pre * (1.0 - sig))).astype(BF16)
    for h in range(2):
        grad[h] = lax.dot_general(
            aggregated,
            grad_pre[:, h * 128 : (h + 1) * 128],
            (((0,), (0,)), ((), ())),
            preferred_element_type=F32,
        ).astype(BF16)


def layer(terms, weight, cotangent):
    return pl.pallas_call(
        layer_kernel,
        out_shape=(
            jax.ShapeDtypeStruct(cotangent.shape, BF16),
            jax.ShapeDtypeStruct((2, BLK, 128), BF16),
        ),
        in_specs=[VMEM, VMEM, VMEM],
        out_specs=(VMEM, VMEM),
        compiler_params=pltpu.CompilerParams(vmem_limit_bytes=4 * 1024 * 1024),
        name="layer",
    )(terms, weight, cotangent)


def exchange(a, axis, groups=None):
    return lax.all_to_all(a, axis, 0, 0, axis_index_groups=groups, tiled=True)


def add_all(terms):
    total = terms[0].astype(F32)
    for i in range(1, terms.shape[0]):
        total = total + terms[i].astype(F32)
    return total


def body(x_feat, weight, tile_values, tile_dst, tile_slot, src_blocks, tile_count, cotangent):
    d_in = x_feat.shape[1]
    xs, fars, nears, cores, cols = SIZES
    with jax.named_scope("ask"):
        pair = src_blocks[:, 0] + 256 * src_blocks[:, 1]
        asked = exchange(jnp.broadcast_to(pair[:, None, None], (cols, 1, 128)), "col")
    with jax.named_scope("pick"):
        picked = pick(asked, x_feat)
    with jax.named_scope("sources"):
        sources = exchange(picked.reshape(cols, 2 * BLK, d_in), "col")
        sources = sources.reshape(cols * 2, BLK, d_in)
    with jax.named_scope("aggregate"):
        core = lax.axis_index("core").astype(jnp.int32).reshape(1)
        mine, theirs = aggregate(tile_dst, tile_slot, tile_count, core, tile_values, sources)
    with jax.named_scope("sum_core"):
        other = lax.ppermute(theirs, "core", [(0, 1), (1, 0)])
        summed = (mine[: other.shape[0]] + other.astype(F32)).astype(BF16)
    with jax.named_scope("sum_x_near"):
        got = exchange(summed.reshape(xs * nears, fars * BLK, d_in), ("x", "near"))
        summed = add_all(got).astype(BF16)
    with jax.named_scope("sum_far"):
        terms = exchange(summed.reshape(fars, BLK, d_in), "far")
    with jax.named_scope("layer"):
        layer_out, grad = layer(terms, weight, cotangent)
    with jax.named_scope("grad_xy"):
        part = add_all(exchange(grad.reshape(32, 8, 128), ("x", "far", "near")))
    with jax.named_scope("grad_core_col"):
        part = jnp.broadcast_to(part[None], (24, 8, 128))
        part = jnp.sum(exchange(part, ("core", "col"), [[12 * c + (z + 6) % 12 for c in (1, 0) for z in range(12)]]), axis=0)
    with jax.named_scope("grad_all"):
        whole = exchange(jnp.broadcast_to(part[None], (32, 8, 128)), ("x", "far", "near"))
        whole = whole.reshape(2, BLK, 128)
        weight_grad = jnp.concatenate([whole[0], whole[1]], axis=1)
    return (layer_out, weight_grad)


def solution(mesh):
    grid = Mesh(mesh.devices.reshape(SIZES), AXES)
    return jax.shard_map(
        body,
        mesh=grid,
        in_specs=(
            P(AXES, None),
            P(),
            P(AXES, None, None),
            P(AXES),
            P(AXES),
            P(AXES, None),
            P(AXES),
            P(AXES, None),
        ),
        out_specs=(P(AXES, None), P()),
        check_vma=False,
    )
```

```python
import jax
import jax.numpy as jnp
from jax import lax
from jax.experimental import pallas as pl
from jax.experimental.pallas import tpu as pltpu
from jax.sharding import Mesh, PartitionSpec as P

BLK = 128
UNROLL = 20
RING = [6 * (i % 2) + i // 2 for i in range(12)]
AXES = ("x", "far", "near", "core", "col")
SIZES = (4, 4, 2, 2, 12)

VMEM = pl.BlockSpec(memory_space=pltpu.VMEM)
SMEM = pl.BlockSpec(memory_space=pltpu.SMEM)
BF16 = jnp.bfloat16
F32 = jnp.float32


def pick_kernel(asked, x_ref, out_ref):
    peers, listed = out_ref.shape[0], out_ref.shape[1]
    for i in range(peers):
        for k in range(listed):
            out_ref[i, k] = x_ref[(asked[RING[i], 0, 0] >> (8 * k)) & 255]


def pick(asked, x_feat):
    peers, listed = SIZES[4], 2
    return pl.pallas_call(
        pick_kernel,
        out_shape=jax.ShapeDtypeStruct((peers, listed, BLK, x_feat.shape[1]), BF16),
        in_specs=[SMEM, VMEM],
        out_specs=VMEM,
        name="pick_blocks",
    )(asked, x_feat.reshape(-1, BLK, x_feat.shape[1]))


def aggregate_kernel(dst, slot, count, core, tiles, sources, acc, theirs):
    half = theirs.shape[0]
    live = count[0]
    me = core[0]
    acc[...] = jnp.zeros_like(acc)

    def group(g, carry):
        for u in range(UNROLL):
            t = g * UNROLL + u
            d = dst[t]
            xy = (d & 0x30) | ((d & 2) << 2) | ((d & 0xC) >> 1)
            place = ((d & 1) ^ me) * half + (xy >> 1)
            place = jnp.where(t < live, place, 2 * half)
            p = slot[t] >> 1
            place_in_ring = 2 * p - jnp.where(p >= 6, 11, 0)
            source = sources[2 * place_in_ring + (slot[t] & 1)]
            acc[place] += jnp.dot(tiles[t], source, preferred_element_type=F32)
        return carry

    lax.fori_loop(0, lax.div(live + (UNROLL - 1), UNROLL), group, 0)
    theirs[...] = acc[pl.ds(half, half)].astype(BF16)


def aggregate(dst, slot, count, core, tiles, sources):
    half = 32
    d_in = sources.shape[-1]
    return pl.pallas_call(
        aggregate_kernel,
        out_shape=(
            jax.ShapeDtypeStruct((2 * half + 1, BLK, d_in), F32),
            jax.ShapeDtypeStruct((half, BLK, d_in), BF16),
        ),
        in_specs=[SMEM, SMEM, SMEM, SMEM, VMEM, VMEM],
        out_specs=(VMEM, VMEM),
        compiler_params=pltpu.CompilerParams(vmem_limit_bytes=16 * 1024 * 1024),
        name="aggregate_tiles",
    )(dst, slot, count, core, tiles, sources)


def layer_kernel(terms, weight, cotangent, out, grad):
    aggregated = add_all(terms).astype(BF16)
    pre = jnp.dot(aggregated, weight[...], preferred_element_type=F32)
    sig = jax.nn.sigmoid(pre)
    out[...] = (pre * sig).astype(BF16)
    grad_pre = (cotangent[...].astype(F32) * sig * (1.0 + pre * (1.0 - sig))).astype(BF16)
    for h in range(2):
        grad[h] = lax.dot_general(
            aggregated,
            grad_pre[:, h * 128 : (h + 1) * 128],
            (((0,), (0,)), ((), ())),
            preferred_element_type=F32,
        ).astype(BF16)


def layer(terms, weight, cotangent):
    return pl.pallas_call(
        layer_kernel,
        out_shape=(
            jax.ShapeDtypeStruct(cotangent.shape, BF16),
            jax.ShapeDtypeStruct((2, BLK, 128), BF16),
        ),
        in_specs=[VMEM, VMEM, VMEM],
        out_specs=(VMEM, VMEM),
        compiler_params=pltpu.CompilerParams(vmem_limit_bytes=4 * 1024 * 1024),
        name="layer",
    )(terms, weight, cotangent)


def exchange(a, axis, groups=None):
    return lax.all_to_all(a, axis, 0, 0, axis_index_groups=groups, tiled=True)


def add_all(terms):
    total = terms[0].astype(F32)
    for i in range(1, terms.shape[0]):
        total = total + terms[i].astype(F32)
    return total


def body(x_feat, weight, tile_values, tile_dst, tile_slot, src_blocks, tile_count, cotangent):
    d_in = x_feat.shape[1]
    xs, fars, nears, cores, cols = SIZES
    with jax.named_scope("ask"):
        pair = src_blocks[:, 0] + 256 * src_blocks[:, 1]
        asked = exchange(jnp.broadcast_to(pair[:, None, None], (cols, 1, 128)), "col")
    with jax.named_scope("pick"):
        picked = pick(asked, x_feat)
    with jax.named_scope("sources"):
        sources = exchange(picked.reshape(cols, 2 * BLK, d_in), "col", [RING])
        sources = sources.reshape(cols * 2, BLK, d_in)
    with jax.named_scope("aggregate"):
        core = lax.axis_index("core").astype(jnp.int32).reshape(1)
        mine, theirs = aggregate(tile_dst, tile_slot, tile_count, core, tile_values, sources)
    with jax.named_scope("sum_core"):
        other = lax.ppermute(theirs, "core", [(0, 1), (1, 0)])
        summed = (mine[: other.shape[0]] + other.astype(F32)).astype(BF16)
    with jax.named_scope("sum_x_near"):
        got = exchange(summed.reshape(xs * nears, fars * BLK, d_in), ("x", "near"))
        summed = add_all(got).astype(BF16)
    with jax.named_scope("sum_far"):
        terms = exchange(summed.reshape(fars, BLK, d_in), "far")
    with jax.named_scope("layer"):
        layer_out, grad = layer(terms, weight, cotangent)
    with jax.named_scope("grad_xy"):
        part = add_all(exchange(grad.reshape(32, 8, 128), ("x", "far", "near")))
    with jax.named_scope("grad_core_col"):
        part = jnp.broadcast_to(part[None], (24, 8, 128))
        part = jnp.sum(exchange(part, ("core", "col"), [[12 * c + (z + 6) % 12 for c in (1, 0) for z in range(12)]]), axis=0)
    with jax.named_scope("grad_all"):
        whole = exchange(jnp.broadcast_to(part[None], (32, 8, 128)), ("x", "far", "near"))
        whole = whole.reshape(2, BLK, 128)
        weight_grad = jnp.concatenate([whole[0], whole[1]], axis=1)
    return (layer_out, weight_grad)


def solution(mesh):
    grid = Mesh(mesh.devices.reshape(SIZES), AXES)
    return jax.shard_map(
        body,
        mesh=grid,
        in_specs=(
            P(AXES, None),
            P(),
            P(AXES, None, None),
            P(AXES),
            P(AXES),
            P(AXES, None),
            P(AXES),
            P(AXES, None),
        ),
        out_specs=(P(AXES, None), P()),
        check_vma=False,
    )
```

```python
import jax
import jax.numpy as jnp
from jax import lax
from jax.experimental import pallas as pl
from jax.experimental.pallas import tpu as pltpu
from jax.sharding import Mesh, PartitionSpec as P

BLK = 128
UNROLL = 40
RING = [6 * (i % 2) + i // 2 for i in range(12)]
NEAR = [4 * (i % 2) + i // 2 for i in range(8)]
AXES = ("x", "far", "near", "core", "col")
SIZES = (4, 4, 2, 2, 12)

VMEM = pl.BlockSpec(memory_space=pltpu.VMEM)
SMEM = pl.BlockSpec(memory_space=pltpu.SMEM)
BF16 = jnp.bfloat16
F32 = jnp.float32


def pick_kernel(asked, x_ref, out_ref):
    peers, listed = out_ref.shape[0], out_ref.shape[1]
    for i in range(peers):
        for k in range(listed):
            out_ref[i, k] = x_ref[(asked[RING[i], 0, 0] >> (8 * k)) & 255]


def pick(asked, x_feat):
    peers, listed = SIZES[4], 2
    return pl.pallas_call(
        pick_kernel,
        out_shape=jax.ShapeDtypeStruct((peers, listed, BLK, x_feat.shape[1]), BF16),
        in_specs=[SMEM, VMEM],
        out_specs=VMEM,
        name="pick_blocks",
    )(asked, x_feat.reshape(-1, BLK, x_feat.shape[1]))


def aggregate_kernel(dst, slot, count, core, tiles, sources, acc, theirs):
    half = theirs.shape[0]
    live = count[0]
    me = core[0]
    acc[...] = jnp.zeros_like(acc)

    def group(g, carry):
        for u in range(UNROLL):
            t = g * UNROLL + u
            d = dst[t]
            inner = (d & 0x10) | ((d & 2) << 2) | ((d & 0x20) >> 3) | ((d & 0xC) >> 2)
            place = ((d & 1) ^ me) * half + inner
            place = jnp.where(t < live, place, 2 * half)
            p = slot[t] >> 1
            place_in_ring = 2 * p - jnp.where(p >= 6, 11, 0)
            source = sources[2 * place_in_ring + (slot[t] & 1)]
            acc[place] += jnp.dot(tiles[t], source, preferred_element_type=F32)
        return carry

    lax.fori_loop(0, lax.div(live + (UNROLL - 1), UNROLL), group, 0)
    theirs[...] = acc[pl.ds(half, half)].astype(BF16)


def aggregate(dst, slot, count, core, tiles, sources):
    half = 32
    d_in = sources.shape[-1]
    return pl.pallas_call(
        aggregate_kernel,
        out_shape=(
            jax.ShapeDtypeStruct((2 * half + 1, BLK, d_in), F32),
            jax.ShapeDtypeStruct((half, BLK, d_in), BF16),
        ),
        in_specs=[SMEM, SMEM, SMEM, SMEM, VMEM, VMEM],
        out_specs=(VMEM, VMEM),
        compiler_params=pltpu.CompilerParams(vmem_limit_bytes=16 * 1024 * 1024),
        name="aggregate_tiles",
    )(dst, slot, count, core, tiles, sources)


def layer_kernel(terms, weight, cotangent, out, grad):
    aggregated = add_all(terms).astype(BF16)
    pre = jnp.dot(aggregated, weight[...], preferred_element_type=F32)
    sig = jax.nn.sigmoid(pre)
    out[...] = (pre * sig).astype(BF16)
    grad_pre = (cotangent[...].astype(F32) * sig * (1.0 + pre * (1.0 - sig))).astype(BF16)
    for h in range(2):
        grad[h] = lax.dot_general(
            aggregated,
            grad_pre[:, h * 128 : (h + 1) * 128],
            (((0,), (0,)), ((), ())),
            preferred_element_type=F32,
        ).astype(BF16)


def layer(terms, weight, cotangent):
    return pl.pallas_call(
        layer_kernel,
        out_shape=(
            jax.ShapeDtypeStruct(cotangent.shape, BF16),
            jax.ShapeDtypeStruct((2, BLK, 128), BF16),
        ),
        in_specs=[VMEM, VMEM, VMEM],
        out_specs=(VMEM, VMEM),
        compiler_params=pltpu.CompilerParams(vmem_limit_bytes=4 * 1024 * 1024),
        name="layer",
    )(terms, weight, cotangent)


def exchange(a, axis, groups=None):
    return lax.all_to_all(a, axis, 0, 0, axis_index_groups=groups, tiled=True)


def add_all(terms):
    total = terms[0].astype(F32)
    for i in range(1, terms.shape[0]):
        total = total + terms[i].astype(F32)
    return total


def body(x_feat, weight, tile_values, tile_dst, tile_slot, src_blocks, tile_count, cotangent):
    d_in = x_feat.shape[1]
    xs, fars, nears, cores, cols = SIZES
    with jax.named_scope("ask"):
        pair = src_blocks[:, 0] + 256 * src_blocks[:, 1]
        asked = exchange(jnp.broadcast_to(pair[:, None, None], (cols, 1, 128)), "col")
    with jax.named_scope("pick"):
        picked = pick(asked, x_feat)
    with jax.named_scope("sources"):
        sources = exchange(picked.reshape(cols, 2 * BLK, d_in), "col", [RING])
        sources = sources.reshape(cols * 2, BLK, d_in)
    with jax.named_scope("aggregate"):
        core = lax.axis_index("core").astype(jnp.int32).reshape(1)
        mine, theirs = aggregate(tile_dst, tile_slot, tile_count, core, tile_values, sources)
    with jax.named_scope("sum_core"):
        other = lax.ppermute(theirs, "core", [(0, 1), (1, 0)])
        summed = (mine[: other.shape[0]] + other.astype(F32)).astype(BF16)
    with jax.named_scope("sum_x_near"):
        got = exchange(summed.reshape(xs * nears, fars * BLK, d_in), ("x", "near"), [NEAR])
        summed = add_all(got).astype(BF16)
    with jax.named_scope("sum_far"):
        terms = exchange(summed.reshape(fars, BLK, d_in), "far")
    with jax.named_scope("layer"):
        layer_out, grad = layer(terms, weight, cotangent)
    with jax.named_scope("grad_xy"):
        part = add_all(exchange(grad.reshape(32, 8, 128), ("x", "far", "near")))
    with jax.named_scope("grad_core_col"):
        part = jnp.broadcast_to(part[None], (24, 8, 128))
        part = jnp.sum(exchange(part, ("core", "col"), [[12 * c + (z + 6) % 12 for c in (1, 0) for z in range(12)]]), axis=0)
    with jax.named_scope("grad_all"):
        whole = exchange(jnp.broadcast_to(part[None], (32, 8, 128)), ("x", "far", "near"))
        whole = whole.reshape(2, BLK, 128)
        weight_grad = jnp.concatenate([whole[0], whole[1]], axis=1)
    return (layer_out, weight_grad)


def solution(mesh):
    grid = Mesh(mesh.devices.reshape(SIZES), AXES)
    return jax.shard_map(
        body,
        mesh=grid,
        in_specs=(
            P(AXES, None),
            P(),
            P(AXES, None, None),
            P(AXES),
            P(AXES),
            P(AXES, None),
            P(AXES),
            P(AXES, None),
        ),
        out_specs=(P(AXES, None), P()),
        check_vma=False,
    )
```

```python
import jax
import jax.numpy as jnp
from jax import lax
from jax.experimental import pallas as pl
from jax.experimental.pallas import tpu as pltpu
from jax.sharding import Mesh, PartitionSpec as P

BLK = 128
UNROLL = 40
RING = [6 * (i % 2) + i // 2 for i in range(12)]
NEAR = [4 * (i % 2) + i // 2 for i in range(8)]
AXES = ("x", "far", "near", "core", "col")
SIZES = (4, 4, 2, 2, 12)

VMEM = pl.BlockSpec(memory_space=pltpu.VMEM)
SMEM = pl.BlockSpec(memory_space=pltpu.SMEM)
BF16 = jnp.bfloat16
F32 = jnp.float32


def pick_kernel(asked, col, x_ref, out_ref):
    peers, listed = out_ref.shape[0], out_ref.shape[1]
    for i in range(peers):
        for k in range(listed):
            out_ref[i, k] = x_ref[(asked[i, 0, col[0]] >> (8 * k)) & 255]


def pick(asked, col, x_feat):
    peers, listed = SIZES[4], 2
    return pl.pallas_call(
        pick_kernel,
        out_shape=jax.ShapeDtypeStruct((peers, listed, BLK, x_feat.shape[1]), BF16),
        in_specs=[SMEM, SMEM, VMEM],
        out_specs=VMEM,
        name="pick_blocks",
    )(asked, col, x_feat.reshape(-1, BLK, x_feat.shape[1]))


def aggregate_kernel(dst, slot, count, core, tiles, sources, acc, theirs):
    half = theirs.shape[0]
    live = count[0]
    me = core[0]
    acc[...] = jnp.zeros_like(acc)

    def group(g, carry):
        for u in range(UNROLL):
            t = g * UNROLL + u
            d = dst[t]
            inner = (d & 0x10) | ((d & 2) << 2) | ((d & 0x20) >> 3) | ((d & 0xC) >> 2)
            place = ((d & 1) ^ me) * half + inner
            place = jnp.where(t < live, place, 2 * half)
            p = slot[t] >> 1
            place_in_ring = 2 * p - jnp.where(p >= 6, 11, 0)
            source = sources[2 * place_in_ring + (slot[t] & 1)]
            acc[place] += jnp.dot(tiles[t], source, preferred_element_type=F32)
        return carry

    lax.fori_loop(0, lax.div(live + (UNROLL - 1), UNROLL), group, 0)
    theirs[...] = acc[pl.ds(half, half)].astype(BF16)


def aggregate(dst, slot, count, core, tiles, sources):
    half = 32
    d_in = sources.shape[-1]
    return pl.pallas_call(
        aggregate_kernel,
        out_shape=(
            jax.ShapeDtypeStruct((2 * half + 1, BLK, d_in), F32),
            jax.ShapeDtypeStruct((half, BLK, d_in), BF16),
        ),
        in_specs=[SMEM, SMEM, SMEM, SMEM, VMEM, VMEM],
        out_specs=(VMEM, VMEM),
        compiler_params=pltpu.CompilerParams(vmem_limit_bytes=16 * 1024 * 1024),
        name="aggregate_tiles",
    )(dst, slot, count, core, tiles, sources)


def layer_kernel(terms, weight, cotangent, out, grad):
    aggregated = add_all(terms).astype(BF16)
    pre = jnp.dot(aggregated, weight[...], preferred_element_type=F32)
    sig = jax.nn.sigmoid(pre)
    out[...] = (pre * sig).astype(BF16)
    grad_pre = (cotangent[...].astype(F32) * sig * (1.0 + pre * (1.0 - sig))).astype(BF16)
    for h in range(2):
        grad[h] = lax.dot_general(
            aggregated,
            grad_pre[:, h * 128 : (h + 1) * 128],
            (((0,), (0,)), ((), ())),
            preferred_element_type=F32,
        ).astype(BF16)


def layer(terms, weight, cotangent):
    return pl.pallas_call(
        layer_kernel,
        out_shape=(
            jax.ShapeDtypeStruct(cotangent.shape, BF16),
            jax.ShapeDtypeStruct((2, BLK, 128), BF16),
        ),
        in_specs=[VMEM, VMEM, VMEM],
        out_specs=(VMEM, VMEM),
        compiler_params=pltpu.CompilerParams(vmem_limit_bytes=4 * 1024 * 1024),
        name="layer",
    )(terms, weight, cotangent)


def exchange(a, axis, groups=None):
    return lax.all_to_all(a, axis, 0, 0, axis_index_groups=groups, tiled=True)


def add_all(terms):
    total = terms[0].astype(F32)
    for i in range(1, terms.shape[0]):
        total = total + terms[i].astype(F32)
    return total


def body(x_feat, weight, tile_values, tile_dst, tile_slot, src_blocks, tile_count, cotangent):
    d_in = x_feat.shape[1]
    xs, fars, nears, cores, cols = SIZES
    with jax.named_scope("ask"):
        pair = src_blocks[:, 0] + 256 * src_blocks[:, 1]
        pair = jnp.pad(pair, (0, 128 - cols))
        asked = exchange(jnp.broadcast_to(pair[None, None], (cols, 1, 128)), "col", [RING])
    with jax.named_scope("pick"):
        col = lax.axis_index("col").astype(jnp.int32).reshape(1)
        picked = pick(asked, col, x_feat)
    with jax.named_scope("sources"):
        sources = exchange(picked.reshape(cols, 2 * BLK, d_in), "col", [RING])
        sources = sources.reshape(cols * 2, BLK, d_in)
    with jax.named_scope("aggregate"):
        core = lax.axis_index("core").astype(jnp.int32).reshape(1)
        mine, theirs = aggregate(tile_dst, tile_slot, tile_count, core, tile_values, sources)
    with jax.named_scope("sum_core"):
        other = lax.ppermute(theirs, "core", [(0, 1), (1, 0)])
        summed = (mine[: other.shape[0]] + other.astype(F32)).astype(BF16)
    with jax.named_scope("sum_x_near"):
        got = exchange(summed.reshape(xs * nears, fars * BLK, d_in), ("x", "near"), [NEAR])
        summed = add_all(got).astype(BF16)
    with jax.named_scope("sum_far"):
        terms = exchange(summed.reshape(fars, BLK, d_in), "far")
    with jax.named_scope("layer"):
        layer_out, grad = layer(terms, weight, cotangent)
    with jax.named_scope("grad_xy"):
        part = add_all(exchange(grad.reshape(32, 8, 128), ("x", "far", "near")))
    with jax.named_scope("grad_core_col"):
        part = jnp.broadcast_to(part[None], (24, 8, 128))
        part = jnp.sum(exchange(part, ("core", "col"), [[12 * c + (z + 6) % 12 for c in (1, 0) for z in range(12)]]), axis=0)
    with jax.named_scope("grad_all"):
        whole = exchange(jnp.broadcast_to(part[None], (32, 8, 128)), ("x", "far", "near"))
        whole = whole.reshape(2, BLK, 128)
        weight_grad = jnp.concatenate([whole[0], whole[1]], axis=1)
    return (layer_out, weight_grad)


def solution(mesh):
    grid = Mesh(mesh.devices.reshape(SIZES), AXES)
    return jax.shard_map(
        body,
        mesh=grid,
        in_specs=(
            P(AXES, None),
            P(),
            P(AXES, None, None),
            P(AXES),
            P(AXES),
            P(AXES, None),
            P(AXES),
            P(AXES, None),
        ),
        out_specs=(P(AXES, None), P()),
        check_vma=False,
    )
```
